128 devices in a mesh: group: 4 (over y), bank: 32 (over z, x, core).
Axes of the slice: x: 4, y: 4, z: 4, core: 2. Of those that a mesh axis runs over, the one named last changes fastest.
Arguments:
- normed_layer_input: bfloat16 [128, 256, 5120], P(('group', 'bank')), may hold values from -6 to 6
- input_times_down: bfloat16 [128, 256, 16], P(('group', 'bank')), may hold values from -6 to 6
- queries: bfloat16 [128, 256, 4096], P(('group', 'bank')), may hold values from -40 to 40
- row_own_keys: bfloat16 [128, 256, 512], P(('group', 'bank')), may hold values from -8 to 8
- row_own_values: bfloat16 [128, 256, 512], P(('group', 'bank')), may hold values from -6 to 6
- output_gradient: bfloat16 [128, 256, 4096], P(('group', 'bank')), may hold values from -6 to 6
- prefix_key_bank: bfloat16 [16, 2048, 512], P(None, ('group', 'bank')), may hold values from -6 to 6
- prefix_value_bank: bfloat16 [16, 2048, 512], P(None, ('group', 'bank')), may hold values from -6 to 6
- live_prefix_length: int32 [16], replicated, may hold values from 512 to 2048, as said below
- tenant: int32 [128], replicated, may hold values from 0 to 15
- tenant_bank_slot: int32 [16], replicated, may hold values from 0 to 15, each once
- tenant_adapter_slot: int32 [16], replicated, may hold values from 0 to 15, each once
- query_up_adapters: bfloat16 [16, 16, 4096], replicated, may hold values from -1.5 to 1.5
Outputs:
- query_grad: bfloat16 [128, 256, 4096], P(('group', 'bank'))
- down_grad: float32 [16, 16, 5120], P('group', None, 'bank')
- up_grad: float32 [16, 16, 4096], P('group', None, 'bank')
The draws below stay inside these ranges and needn't reach their ends.
Inputs may be any that keep to these rules, and one draw needn't show every extreme that they name: `live_prefix_length`: some tenant's whole prefix is live.
All inputs are finite; a program needn't handle non-finite values.
Results may differ from the reference program's by a relative error of at most 0.0064.
Values may be sent and summed in bfloat16 or wider, within the bound.
No kernel may reach another device: no remote copies, remote signals or barrier semaphores. Data moves between devices by JAX's collectives and lax.ppermute only.
A program may use at most 192 MiB of HBM per device.

```python
import math
import jax
import jax.numpy as jnp
import numpy as np
from jax import lax

D = 5120
QUERY_HEAD_COUNT = 32
KV_HEADS = 4
HEAD_WIDTH = 128
ADAPTER_RANK = 16
SEQ = 256
PREFIX = 2048
TENANT_COUNT = 16
ROWS = 128


def shared_keys(key):
    raw = jax.random.normal(key, (ROWS, SEQ, KV_HEADS, HEAD_WIDTH), jnp.float32)
    return jnp.clip(raw, -4.0, 4.0)


def draw_row_own_keys(key, part):
    base_keys = shared_keys(key)
    result = base_keys
    return result.reshape(ROWS, SEQ, KV_HEADS * HEAD_WIDTH).astype(jnp.bfloat16)


def draw_queries(key, part):
    key = jax.random.fold_in(key, 13)
    group_size = QUERY_HEAD_COUNT // KV_HEADS
    fresh = jnp.clip(jax.random.normal(key, (ROWS, SEQ, KV_HEADS, group_size, HEAD_WIDTH), jnp.float32), -4.0, 4.0)
    result = fresh
    return result.reshape(ROWS, SEQ, QUERY_HEAD_COUNT * HEAD_WIDTH).astype(jnp.bfloat16)


def draw_live_prefix_length(key, part):
    key = jax.random.fold_in(key, 17)
    drawn = jax.random.randint(key, (TENANT_COUNT,), PREFIX // 4, PREFIX + 1)
    longest = jax.random.randint(jax.random.fold_in(key, 1), (), 0, TENANT_COUNT)
    return jnp.where(jnp.arange(TENANT_COUNT) == longest, PREFIX, drawn).astype(jnp.int32)


def place_ends(entries, stream_key, least, top_value):
    index_at = [jax.random.randint(jax.random.fold_in(stream_key, axis), (), 0, length) for axis, length in enumerate(entries.shape)]
    widest = entries.shape.index(max(entries.shape))
    next_to = index_at[:widest] + [(index_at[widest] + 1) % entries.shape[widest]] + index_at[widest + 1:]
    return entries.at[tuple(index_at)].set(least).at[tuple(next_to)].set(top_value)


def level_of(stream_key, dims, cuts, least, high):
    def one(dim, shards_of):
        heights = jax.random.uniform(jax.random.fold_in(jax.random.fold_in(stream_key, 6), dim), (shards_of,), jnp.float32, least / len(cuts), high / len(cuts))
        return jnp.repeat(jnp.exp(heights), dims[dim] // shards_of).reshape((-1,) + (1,) * (len(dims) - dim - 1))

    loudness = one(*cuts[0])
    for cut in cuts[1:]:
        loudness = loudness * one(*cut)
    return loudness


def cumulative_ranks(amount, skew):
    portions = [(1 << 20) // math.isqrt(standing ** skew) + 1 for standing in range(1, amount + 1)]
    scale = 1 + sum(portions) // (1 << 30)
    return np.cumsum(np.array([max(1, weight // scale) for weight in portions]))


def ranked_ids(rng, shape, count, skew):
    grid = cumulative_ranks(count, skew)
    ticket = jax.random.randint(jax.random.fold_in(rng, 1), shape, 0, int(grid[count - 1]))
    rank = jnp.searchsorted(jnp.asarray(grid, jnp.int32), ticket, side="right")
    return jax.random.permutation(jax.random.fold_in(rng, 2), count)[rank].astype(jnp.int32)


def centred(own_key, shape, deviation, most, cuts=(), held_as=jnp.bfloat16):
    values = deviation * jax.random.normal(own_key, shape, jnp.float32)
    if cuts:
        values = values * level_of(own_key, shape, cuts, -0.22, 0.18)
    return jnp.clip(values, -most, most).astype(held_as)


def setup_inputs(seed: int = 0) -> dict:
    streams_of = jax.random.split(jax.random.key(seed), 14)
    return {
        "normed_layer_input": centred(streams_of[0], (ROWS, SEQ, D), 1.0, 6.0, ((0, 128),)),
        "input_times_down": centred(streams_of[1], (ROWS, SEQ, ADAPTER_RANK), 1.0, 6.0, ((0, 128),)),
        "queries": draw_queries(jax.random.fold_in(streams_of[13], 71), 0),
        "row_own_keys": draw_row_own_keys(jax.random.fold_in(streams_of[13], 71), 0),
        "row_own_values": centred(streams_of[4], (ROWS, SEQ, KV_HEADS * HEAD_WIDTH), 1.0, 6.0, ((0, 128),)),
        "output_gradient": centred(streams_of[5], (ROWS, SEQ, QUERY_HEAD_COUNT * HEAD_WIDTH), 1.0, 6.0, ((0, 128),)),
        "prefix_key_bank": centred(streams_of[6], (TENANT_COUNT, PREFIX, KV_HEADS * HEAD_WIDTH), 1.0, 6.0, ((1, 128),)),
        "prefix_value_bank": centred(streams_of[7], (TENANT_COUNT, PREFIX, KV_HEADS * HEAD_WIDTH), 1.0, 6.0, ((1, 128),)),
        "live_prefix_length": draw_live_prefix_length(jax.random.fold_in(streams_of[13], 71), 0),
        "tenant": place_ends(ranked_ids(streams_of[9], (ROWS,), TENANT_COUNT, 2), jax.random.fold_in(streams_of[9], 3), 0, TENANT_COUNT - 1).astype(jnp.int32),
        "tenant_bank_slot": jax.random.permutation(streams_of[10], TENANT_COUNT).astype(jnp.int32),
        "tenant_adapter_slot": jax.random.permutation(streams_of[11], TENANT_COUNT).astype(jnp.int32),
        "query_up_adapters": centred(streams_of[12], (TENANT_COUNT, ADAPTER_RANK, QUERY_HEAD_COUNT * HEAD_WIDTH), ADAPTER_RANK ** -0.5, 1.5),
    }


adapter_scale = 2.0
masked = -1.0e30


def split_heads(block):
    seq_len = block.shape[0]
    group_size = QUERY_HEAD_COUNT // KV_HEADS
    shaped = block.reshape(seq_len, KV_HEADS, group_size, HEAD_WIDTH)
    return shaped.transpose(1, 2, 0, 3).reshape(KV_HEADS, group_size * seq_len, HEAD_WIDTH)


def merge_heads(block):
    group_size = QUERY_HEAD_COUNT // KV_HEADS
    seq_len = block.shape[1] // group_size
    shaped = block.reshape(KV_HEADS, group_size, seq_len, HEAD_WIDTH)
    return shaped.transpose(2, 0, 1, 3).reshape(seq_len, QUERY_HEAD_COUNT * HEAD_WIDTH)


def key_heads(block):
    return block.reshape(-1, KV_HEADS, HEAD_WIDTH).transpose(1, 0, 2)


def reference(normed_layer_input, input_times_down, queries, row_own_keys, row_own_values, output_gradient, prefix_key_bank, prefix_value_bank, live_prefix_length, tenant, tenant_bank_slot, tenant_adapter_slot, query_up_adapters):
    group_size = QUERY_HEAD_COUNT // KV_HEADS
    score_scale = HEAD_WIDTH ** -0.5
    query_pos = jnp.tile(jnp.arange(SEQ), group_size)
    causal = query_pos[:, None] >= jnp.arange(SEQ)[None, :]

    def per_row(totals, inputs):
        down_total, up_total = totals
        input_of_row, row_down_product, row_query, row_key, row_value, row_grad, row_tenant = inputs
        bank_row = tenant_bank_slot[row_tenant]
        owning_slot = tenant_adapter_slot[row_tenant]
        length = live_prefix_length[row_tenant]
        all_keys = key_heads(jnp.concatenate([prefix_key_bank[bank_row], row_key], 0)).astype(jnp.float32)
        all_values = key_heads(jnp.concatenate([prefix_value_bank[bank_row], row_value], 0)).astype(jnp.float32)
        query_heads = split_heads(row_query).astype(jnp.float32)
        grad_heads = split_heads(row_grad).astype(jnp.float32)
        prefix_seen = jnp.broadcast_to((jnp.arange(PREFIX) < length)[None, :], (group_size * SEQ, PREFIX))
        visible = jnp.concatenate([prefix_seen, causal], 1)
        scores = jnp.einsum("gqd,gkd->gqk", query_heads, all_keys) * score_scale
        scores = jnp.where(visible[None], scores, masked)
        row_max = jnp.max(scores, -1, keepdims=True)
        log_total = row_max + jnp.log(jnp.sum(jnp.exp(scores - row_max), -1, keepdims=True))
        weights = jnp.exp(scores - log_total)
        weights_low = lax.optimization_barrier(weights.astype(jnp.bfloat16)).astype(jnp.float32)
        attn_out = jnp.einsum("gqk,gkd->gqd", weights_low, all_values)
        delta_term = jnp.sum(grad_heads * attn_out, -1, keepdims=True)
        prob_grad = jnp.einsum("gqd,gkd->gqk", grad_heads, all_values)
        score_grad = lax.optimization_barrier((weights * (prob_grad - delta_term)).astype(jnp.bfloat16)).astype(jnp.float32)
        query_heads_grad = (jnp.einsum("gqk,gkd->gqd", score_grad, all_keys) * score_scale).astype(jnp.bfloat16)
        flat_gradient = merge_heads(query_heads_grad)
        adapter_middle = jnp.dot(flat_gradient, query_up_adapters[owning_slot].T, preferred_element_type=jnp.float32).astype(jnp.bfloat16)
        first_row = adapter_scale * jnp.dot(adapter_middle.T, input_of_row, preferred_element_type=jnp.float32)
        second_row = adapter_scale * jnp.dot(row_down_product.T, flat_gradient, preferred_element_type=jnp.float32)
        return (down_total.at[owning_slot].add(first_row), up_total.at[owning_slot].add(second_row)), flat_gradient

    initial = (jnp.zeros((TENANT_COUNT, ADAPTER_RANK, D), jnp.float32), jnp.zeros((TENANT_COUNT, ADAPTER_RANK, QUERY_HEAD_COUNT * HEAD_WIDTH), jnp.float32))
    sums, query_grad = lax.scan(per_row, initial, (normed_layer_input, input_times_down, queries, row_own_keys, row_own_values, output_gradient, tenant))
    return query_grad, sums[0], sums[1]
```

```python
import math

import jax
import jax.numpy as jnp
from jax import lax
from jax.experimental import pallas as pl
from jax.experimental.pallas import tpu as pltpu
from jax.sharding import PartitionSpec as P

SEQ = 256
PREFIX = 2048
HEAD = 128
KV_HEADS = 4
GROUP = 8
RANK = 16
KEY_BLOCK = 256
BLOCKS = PREFIX // KEY_BLOCK
ALL_KEYS = PREFIX + SEQ
LEAST_LIVE = 512
SLOTS = 16
MASKED = -1e30
SCALE = HEAD**-0.5
SCALE2 = SCALE * math.log2(math.e)
ADAPTER_SCALE = 2.0
ROWS_AT_ONCE = 16
UP = 128
DOWN = 160
TERM = 384


def dot(a, b, a_dim, b_dim):
    return lax.dot_general(
        a, b, (((a_dim,), (b_dim,)), ((), ())), preferred_element_type=jnp.float32
    )


def attention_kernel(
    own, tenant, lengths, adapter_slot,
    q_ref, grad_ref, key_ref, value_ref, own_key_ref, own_value_ref, adapter_ref, mid_in_ref, x_ref,
    dq_ref, t0_ref, t1_ref, t2_ref, t3_ref,
    scores, probs, score_grad, bias, mid_sum, down,
):
    g = pl.program_id(0)
    length = lengths[tenant[own[0]]]
    position = lax.broadcasted_iota(jnp.int32, bias.shape, 1)
    bias[...] = jnp.where(position < length, 0.0, MASKED)

    def block(prefix_ref, own_ref, j):
        return prefix_ref[j * KEY_BLOCK : (j + 1) * KEY_BLOCK, :] if j < BLOCKS else own_ref[...]

    def head(h, carry):
        columns = pl.ds(pl.multiple_of(h * HEAD, HEAD), HEAD)
        q = q_ref[:, columns]
        grad = grad_ref[:, columns]
        for j in range(BLOCKS + 1):
            s = dot(q, block(key_ref, own_key_ref, j), 1, 1)
            if j == BLOCKS:
                row = lax.broadcasted_iota(jnp.int32, (SEQ, SEQ), 0)
                column = lax.broadcasted_iota(jnp.int32, (SEQ, SEQ), 1)
                s = jnp.where(column <= row, s, MASKED)
            elif (j + 1) * KEY_BLOCK > LEAST_LIVE:
                s = s + bias[0:1, j * KEY_BLOCK : (j + 1) * KEY_BLOCK]
            scores[:, j * KEY_BLOCK : (j + 1) * KEY_BLOCK] = s
        for j in range(BLOCKS + 1):
            probs[:, j * KEY_BLOCK : (j + 1) * KEY_BLOCK] = dot(
                grad, block(value_ref, own_value_ref, j), 1, 1
            )
        for r in range(0, SEQ, ROWS_AT_ONCE):
            rows = slice(r, r + ROWS_AT_ONCE)
            s = scores[rows, :]
            top = jnp.max(s, axis=-1, keepdims=True)
            e = jnp.exp2(s * SCALE2 - top * SCALE2)
            weights = e * (1.0 / jnp.sum(e, axis=-1, keepdims=True))
            weights_low = weights.astype(jnp.bfloat16).astype(jnp.float32)
            prob_grad = probs[rows, :]
            delta = jnp.sum(weights_low * prob_grad, axis=-1, keepdims=True)
            score_grad[rows, :] = (weights * (prob_grad - delta)).astype(jnp.bfloat16)
        total = dot(score_grad[:, :PREFIX], key_ref[...], 1, 0)
        total += dot(score_grad[:, PREFIX:], own_key_ref[...], 1, 0)
        dq_ref[:, columns] = (total * SCALE).astype(jnp.bfloat16)
        return carry

    lax.fori_loop(0, GROUP, head, 0)

    @pl.when(g == 0)
    def _():
        mid_sum[...] = jnp.zeros_like(mid_sum)

    dq = dq_ref[...]
    mid_sum[...] += dot(dq, adapter_ref[0], 1, 1)
    up = (ADAPTER_SCALE * dot(mid_in_ref[...], dq, 0, 0)).astype(jnp.bfloat16)

    bank = lax.rem(own[0], 32)
    my_z, my_x, my_core = bank // 8, lax.rem(bank // 2, 4), lax.rem(bank, 2)
    terms = (t0_ref, t1_ref, t2_ref, t3_ref)

    def place(b, write):
        z, x, core = b // 8, lax.rem(b // 2, 4), lax.rem(b, 2)
        far_z, far_x = lax.rem(z - my_z + 4, 4), lax.rem(x - my_x + 4, 4)
        far_core = jnp.where(core == my_core, 0, 1)
        at = far_z * 2 + far_core
        for k in range(4):

            @pl.when(far_x == k)
            def _():
                write(terms[k], at)

    for i in range(GROUP):
        def write_up(ref, at, i=i):
            ref[at, :, 0:UP] = up[:, i * UP : (i + 1) * UP]

        place(g * GROUP + i, write_up)

    @pl.when(g == KV_HEADS - 1)
    def _():
        mid = mid_sum[...].astype(jnp.bfloat16)
        down[...] = ADAPTER_SCALE * dot(mid, x_ref[...], 0, 0)
        for b in range(32):
            def write_down(ref, at, b=b):
                ref[at, :, UP : UP + DOWN] = down[:, b * DOWN : (b + 1) * DOWN].astype(jnp.bfloat16)
                ref[at, :, UP + DOWN :] = jnp.zeros((RANK, TERM - UP - DOWN), jnp.bfloat16)

            place(jnp.int32(b), write_down)


def attention(own, tenant, lengths, adapter_slot, q, grad, pairs, own_key, own_value, adapters, mid_in, x):
    def wide(shape):
        return pl.BlockSpec(shape, lambda g, *_: (0, g))

    def whole(shape):
        return pl.BlockSpec(shape, lambda g, *_: (0,) * len(shape))

    def adapter_at(g, own, tenant, lengths, adapter_slot):
        return (adapter_slot[tenant[own[0]]], 0, g)

    term = jax.ShapeDtypeStruct((8, RANK, TERM), jnp.bfloat16)
    return pl.pallas_call(
        attention_kernel,
        out_shape=(jax.ShapeDtypeStruct(q.shape, jnp.bfloat16),) + (term,) * 4,
        grid_spec=pltpu.PrefetchScalarGridSpec(
            num_scalar_prefetch=4,
            grid=(KV_HEADS,),
            in_specs=[
                wide((SEQ, GROUP * HEAD)),
                wide((SEQ, GROUP * HEAD)),
                wide((PREFIX, HEAD)),
                pl.BlockSpec((PREFIX, HEAD), lambda g, *_: (0, KV_HEADS + g)),
                wide((SEQ, HEAD)),
                wide((SEQ, HEAD)),
                pl.BlockSpec((1, RANK, GROUP * HEAD), adapter_at),
                whole(mid_in.shape),
                whole(x.shape),
            ],
            out_specs=(wide((SEQ, GROUP * HEAD)),) + (whole(term.shape),) * 4,
            scratch_shapes=[
                pltpu.VMEM((SEQ, ALL_KEYS), jnp.float32),
                pltpu.VMEM((SEQ, ALL_KEYS), jnp.float32),
                pltpu.VMEM((SEQ, ALL_KEYS), jnp.bfloat16),
                pltpu.VMEM((8, PREFIX), jnp.float32),
                pltpu.VMEM((SEQ, RANK), jnp.float32),
                pltpu.VMEM((RANK, x.shape[1]), jnp.float32),
            ],
        ),
        compiler_params=pltpu.CompilerParams(vmem_limit_bytes=48 << 20),
        cost_estimate=pl.CostEstimate(flops=15_000_000_000, bytes_accessed=16_000_000, transcendentals=19_000_000),
        name="attention",
    )(own, tenant, lengths, adapter_slot, q, grad, pairs, pairs, own_key, own_value, adapters, mid_in, x)


def sum_kernel(own, slots, near_ref, far_ref, a0_ref, a1_ref, a2_ref, a3_ref, total):
    total[...] = jnp.zeros_like(total)
    for half, ref in enumerate((near_ref, far_ref)):
        for i in range(16):
            slot = slots[half * 16 + i]
            total[slot] += ref[i].astype(jnp.float32)
    mine = own[0] // 32
    for k, ref in enumerate((a0_ref, a1_ref, a2_ref, a3_ref)):
        first = lax.rem(mine + k, 4) * 4
        for i in range(4):
            ref[i] = total[first + i]


def sum_terms(own, slots, near, far):
    out = jax.ShapeDtypeStruct((4, RANK, TERM), jnp.float32)
    return pl.pallas_call(
        sum_kernel,
        out_shape=(out,) * 4,
        grid_spec=pltpu.PrefetchScalarGridSpec(
            num_scalar_prefetch=2,
            grid=(1,),
            in_specs=[pl.BlockSpec((16, RANK, TERM), lambda i, *_: (0, 0, 0))] * 2,
            out_specs=[pl.BlockSpec((4, RANK, TERM), lambda i, *_: (0, 0, 0))] * 4,
            scratch_shapes=[pltpu.VMEM((SLOTS, RANK, TERM), jnp.float32)],
        ),
        name="sum_terms",
    )(own, slots, near, far)


def bank_at(z, x, core):
    return (z % 4) * 8 + (x % 4) * 2 + core


BANKS = [(z, x, c) for z in range(4) for x in range(4) for c in range(2)]


def to_x(k):
    return [(bank_at(z, x, c), bank_at(z, x + k, c)) for z, x, c in BANKS]


def to_z(k):
    return [(bank_at(z, x, c), bank_at(z + k, x, c)) for z, x, c in BANKS]


TO_CORE = [(bank_at(z, x, c), bank_at(z, x, 1 - c)) for z, x, c in BANKS]


def body(
    normed_layer_input,
    input_times_down,
    queries,
    row_own_keys,
    row_own_values,
    output_gradient,
    prefix_key_bank,
    prefix_value_bank,
    live_prefix_length,
    tenant,
    tenant_bank_slot,
    tenant_adapter_slot,
    query_up_adapters,
):
    own = lax.axis_index(("group", "bank")).astype(jnp.int32)
    own1 = own[None]
    share = jnp.concatenate([prefix_key_bank, prefix_value_bank], -1)
    send = share[tenant_bank_slot[tenant]]
    got = lax.all_to_all(send, ("group", "bank"), split_axis=0, concat_axis=0, tiled=True)
    pairs = got.reshape(PREFIX, -1)
    dq, *terms = attention(
        own1, tenant, live_prefix_length, tenant_adapter_slot, queries[0], output_gradient[0],
        pairs, row_own_keys[0], row_own_values[0], query_up_adapters, input_times_down[0],
        normed_layer_input[0],
    )
    by_x = [terms[0]] + [lax.ppermute(terms[k], "bank", to_x(k)) for k in range(1, 4)]
    held = jnp.stack([t.reshape(4, 2, RANK, TERM) for t in by_x], 1)
    by_z = [held[0]] + [lax.ppermute(held[k], "bank", to_z(k)) for k in range(1, 4)]
    held = jnp.stack(by_z, 0)
    near = held[:, :, 0].reshape(16, RANK, TERM)
    far = lax.ppermute(held[:, :, 1].reshape(16, RANK, TERM), "bank", TO_CORE)
    group, bank = own // 32, own % 32
    my_z, my_x, my_core = bank // 8, (bank // 2) % 4, bank % 2
    back = jnp.arange(4, dtype=jnp.int32)
    row_z = ((my_z - back) % 4)[None, :, None]
    row_x = ((my_x - back) % 4)[None, None, :]
    row_core = jnp.stack([my_core, 1 - my_core])[:, None, None]
    rows = (group * 32 + row_z * 8 + row_x * 2 + row_core).reshape(32)
    slots = tenant_adapter_slot[tenant[rows]]
    sums = sum_terms(own1, slots, near, far)
    for k in range(1, 4):
        part = lax.ppermute(sums[k], "group", [(i, (i + k) % 4) for i in range(4)])
        total = sums[0] + part if k == 1 else total + part
    return dq[None], total[:, :, UP : UP + DOWN], total[:, :, :UP]


def solution(mesh):
    rows = P(("group", "bank"), None, None)
    return jax.shard_map(
        body,
        mesh=mesh,
        in_specs=(rows,) * 6 + (P(None, ("group", "bank"), None),) * 2 + (P(),) * 5,
        out_specs=(rows, P("group", None, "bank"), P("group", None, "bank")),
        check_vma=False,
    )
```

```python
import functools
import math

import jax
import jax.numpy as jnp
from jax import lax
from jax.experimental import pallas as pl
from jax.experimental.pallas import tpu as pltpu
from jax.sharding import PartitionSpec as P

SEQ = 256
PREFIX = 2048
HEAD = 128
KV_HEADS = 4
GROUP = 8
RANK = 16
KEY_BLOCK = 256
BLOCKS = PREFIX // KEY_BLOCK
ALL_KEYS = PREFIX + SEQ
LEAST_LIVE = 512
SLOTS = 16
MASKED = -1e30
SCALE = HEAD**-0.5
SCALE2 = SCALE * math.log2(math.e)
ADAPTER_SCALE = 2.0
ROWS_AT_ONCE = 16
UP = 128
DOWN = 160
TERM = 384
BANKS = 32
PART = 2


def lookup(table, position):
    matches = position[..., None] == jnp.arange(table.shape[0], dtype=jnp.int32)
    return jnp.sum(jnp.where(matches, table, 0), -1)


def dot(a, b, a_dim, b_dim):
    return lax.dot_general(
        a, b, (((a_dim,), (b_dim,)), ((), ())), preferred_element_type=jnp.float32
    )


def interleave(a, b):
    mixed, i, j = [], 0, 0
    while i < len(a) or j < len(b):
        if j == len(b) or (i < len(a) and i * len(b) <= j * len(a)):
            mixed.append(a[i])
            i += 1
        else:
            mixed.append(b[j])
            j += 1
    return mixed


def run(steps):
    for step in steps:
        step()


def attention_kernel(
    last,
    own, tenant, lengths, adapter_slot,
    q_ref, grad_ref, key_ref, value_ref, own_key_ref, own_value_ref, adapter_ref, mid_in_ref,
    *refs,
):
    if last:
        _, mid_so_far, up_so_far, x_ref, dq_ref, term_ref, *scratch = refs
    else:
        dq_ref, mid_ref, up_ref, *scratch = refs
    scores0, scores1, probs0, probs1, grads0, grads1, bias, partial, mid_sum, down = scratch
    g = pl.program_id(0)
    scores, probs, grads = (scores0, scores1), (probs0, probs1), (grads0, grads1)
    length = lengths[tenant[own[0]]]
    position = lax.broadcasted_iota(jnp.int32, bias.shape, 1)
    bias[...] = jnp.where(position < length, 0.0, MASKED)
    tiles = [(j, j + KEY_BLOCK) for j in range(0, ALL_KEYS, KEY_BLOCK)]

    def block(prefix_ref, own_ref, a, b):
        return prefix_ref[a:b, :] if a < PREFIX else own_ref[...]

    def pair(ref, p):
        return jnp.concatenate(
            [ref[:, i * HEAD : (i + 1) * HEAD] for i in (2 * p, 2 * p + 1)], axis=0
        )

    def front(p, s):
        q, grad = pair(q_ref, p), pair(grad_ref, p)

        def score(a, b):
            scores[s][:, a:b] = dot(q, block(key_ref, own_key_ref, a, b), 1, 1)

        def prob(a, b):
            probs[s][:, a:b] = dot(grad, block(value_ref, own_value_ref, a, b), 1, 1)

        return [functools.partial(f, a, b) for f in (score, prob) for a, b in tiles]

    def soft(s):
        def rows_at(r):
            rows = slice(r, r + ROWS_AT_ONCE)
            x = scores[s][rows, :]
            row = lax.broadcasted_iota(jnp.int32, (ROWS_AT_ONCE, SEQ), 0) + r % SEQ
            column = lax.broadcasted_iota(jnp.int32, (ROWS_AT_ONCE, SEQ), 1)
            x = jnp.concatenate(
                [
                    x[:, :LEAST_LIVE],
                    x[:, LEAST_LIVE:PREFIX] + bias[0:1, LEAST_LIVE:],
                    jnp.where(column <= row, x[:, PREFIX:], MASKED),
                ],
                axis=1,
            )
            top = jnp.max(x, axis=-1, keepdims=True)
            e = jnp.exp2(x * SCALE2 - top * SCALE2)
            inverse = 1.0 / jnp.sum(e, axis=-1, keepdims=True)
            prob_grad = probs[s][rows, :]
            delta = jnp.sum(e * prob_grad, axis=-1, keepdims=True) * inverse
            grads[s][rows, :] = ((e * inverse) * (prob_grad - delta)).astype(jnp.bfloat16)

        return [functools.partial(rows_at, r) for r in range(0, 2 * SEQ, ROWS_AT_ONCE)]

    def back(p, s):
        def part(i, a, b):
            x = dot(grads[s][:, a:b], block(key_ref, own_key_ref, a, b), 1, 0)
            if i:
                x += partial[...]
            if b < ALL_KEYS:
                partial[...] = x
            else:
                x = (x * SCALE).astype(jnp.bfloat16)
                for k in range(2):
                    dq_ref[:, (2 * p + k) * HEAD : (2 * p + k + 1) * HEAD] = x[k * SEQ : (k + 1) * SEQ]

        return [functools.partial(part, i, a, b) for i, (a, b) in enumerate(tiles)]

    run(front(0, 0))
    run(interleave(front(1, 1), soft(0)))
    run(interleave(front(2, 0) + back(0, 0), soft(1)))
    run(interleave(front(3, 1) + back(1, 1), soft(0)))
    run(interleave(back(2, 0), soft(1)))
    run(back(3, 1))

    @pl.when(g == 0)
    def _():
        mid_sum[...] = mid_so_far[...] if last else jnp.zeros_like(mid_sum)

    dq = dq_ref[...]
    mid_sum[...] += dot(dq, adapter_ref[0], 1, 1)
    up = (ADAPTER_SCALE * dot(mid_in_ref[...], dq, 0, 0)).astype(jnp.bfloat16)
    for i in range(GROUP):
        piece = up[:, i * UP : (i + 1) * UP]
        if last:
            term_ref[BANKS // 2 + g * GROUP + i, :, 0:UP] = piece
        else:
            up_ref[i] = piece

    @pl.when(g == PART - 1)
    def _():
        if last:
            mid = mid_sum[...].astype(jnp.bfloat16)
            down[...] = ADAPTER_SCALE * dot(mid, x_ref[...], 0, 0)
            for b in range(BANKS):
                if b < BANKS // 2:
                    term_ref[b, :, 0:UP] = up_so_far[b]
                term_ref[b, :, UP : UP + DOWN] = down[:, b * DOWN : (b + 1) * DOWN].astype(jnp.bfloat16)
                term_ref[b, :, UP + DOWN :] = jnp.zeros((RANK, TERM - UP - DOWN), jnp.bfloat16)
        else:
            mid_ref[...] = mid_sum[...]


def attention(first, own, tenant, lengths, adapter_slot, q, grad, pairs, own_key, own_value, adapters, mid_in, earlier):
    last = bool(earlier)

    def wide(shape):
        return pl.BlockSpec(shape, lambda g, *_: (0, first + g))

    def whole(shape):
        return pl.BlockSpec(shape, lambda g, *_: (0,) * len(shape))

    def adapter_at(g, own, tenant, lengths, adapter_slot):
        return (adapter_slot[tenant[own[0]]], 0, first + g)

    dq = jax.ShapeDtypeStruct(q.shape, jnp.bfloat16)
    if last:
        out_shape = (dq, jax.ShapeDtypeStruct((BANKS, RANK, TERM), jnp.bfloat16))
        out_specs = (wide((SEQ, GROUP * HEAD)), whole((BANKS, RANK, TERM)))
        more = [pl.BlockSpec(memory_space=pl.ANY)] + [whole(e.shape) for e in earlier[1:]]
    else:
        out_shape = (
            dq,
            jax.ShapeDtypeStruct((SEQ, RANK), jnp.float32),
            jax.ShapeDtypeStruct((BANKS // 2, RANK, UP), jnp.bfloat16),
        )
        out_specs = (
            wide((SEQ, GROUP * HEAD)),
            whole((SEQ, RANK)),
            pl.BlockSpec((GROUP, RANK, UP), lambda g, *_: (g, 0, 0)),
        )
        more = []
    return pl.pallas_call(
        functools.partial(attention_kernel, last),
        out_shape=out_shape,
        grid_spec=pltpu.PrefetchScalarGridSpec(
            num_scalar_prefetch=4,
            grid=(PART,),
            in_specs=[
                wide((SEQ, GROUP * HEAD)),
                wide((SEQ, GROUP * HEAD)),
                pl.BlockSpec((PREFIX, HEAD), lambda g, *_: (0, g)),
                pl.BlockSpec((PREFIX, HEAD), lambda g, *_: (0, PART + g)),
                wide((SEQ, HEAD)),
                wide((SEQ, HEAD)),
                pl.BlockSpec((1, RANK, GROUP * HEAD), adapter_at),
                whole(mid_in.shape),
                *more,
            ],
            out_specs=out_specs,
            scratch_shapes=[
                *[pltpu.VMEM((2 * SEQ, ALL_KEYS), jnp.float32)] * 4,
                *[pltpu.VMEM((2 * SEQ, ALL_KEYS), jnp.bfloat16)] * 2,
                pltpu.VMEM((8, PREFIX), jnp.float32),
                pltpu.VMEM((2 * SEQ, HEAD), jnp.float32),
                pltpu.VMEM((SEQ, RANK), jnp.float32),
                pltpu.VMEM((RANK, BANKS * DOWN), jnp.float32),
            ],
        ),
        input_output_aliases={12: 0} if last else {},
        compiler_params=pltpu.CompilerParams(vmem_limit_bytes=56 << 20),
        cost_estimate=pl.CostEstimate(flops=15_000_000_000, bytes_accessed=8_000_000, transcendentals=10_000_000),
        name="attention_last" if last else "attention_first",
    )(own, tenant, lengths, adapter_slot, q, grad, pairs, pairs, own_key, own_value, adapters, mid_in, *earlier)


def sum_kernel(own, tenant, adapter_slot, terms_ref, a0_ref, a1_ref, a2_ref, a3_ref, total):
    total[...] = jnp.zeros_like(total)
    mine = own[0] // BANKS
    for i in range(BANKS):
        slot = adapter_slot[tenant[mine * BANKS + i]]
        total[slot] += terms_ref[i].astype(jnp.float32)
    for k, ref in enumerate((a0_ref, a1_ref, a2_ref, a3_ref)):
        start = lax.rem(mine + k, 4) * 4
        for i in range(4):
            ref[i] = total[start + i].astype(ref.dtype)


def sum_terms(own, tenant, adapter_slot, terms):
    shape = (4, RANK, TERM)
    return pl.pallas_call(
        sum_kernel,
        out_shape=[
            jax.ShapeDtypeStruct(shape, jnp.bfloat16 if k else jnp.float32) for k in range(4)
        ],
        grid_spec=pltpu.PrefetchScalarGridSpec(
            num_scalar_prefetch=3,
            grid=(1,),
            in_specs=[pl.BlockSpec(terms.shape, lambda i, *_: (0, 0, 0))],
            out_specs=[pl.BlockSpec(shape, lambda i, *_: (0, 0, 0))] * 4,
            scratch_shapes=[pltpu.VMEM((SLOTS, RANK, TERM), jnp.float32)],
        ),
        name="sum_terms",
    )(own, tenant, adapter_slot, terms)


def body(
    normed_layer_input,
    input_times_down,
    queries,
    row_own_keys,
    row_own_values,
    output_gradient,
    prefix_key_bank,
    prefix_value_bank,
    live_prefix_length,
    tenant,
    tenant_bank_slot,
    tenant_adapter_slot,
    query_up_adapters,
):
    own = lax.axis_index(("group", "bank")).astype(jnp.int32)[None]
    bank_slot = lookup(tenant_bank_slot, tenant)
    width = PART * HEAD
    pairs = []
    for first in range(0, KV_HEADS, PART):
        columns = slice(first * HEAD, first * HEAD + width)
        share = jnp.concatenate([prefix_key_bank[:, :, columns], prefix_value_bank[:, :, columns]], -1)
        got = lax.all_to_all(share[bank_slot], ("group", "bank"), split_axis=0, concat_axis=0, tiled=True)
        pairs.append(got.reshape(PREFIX, 2 * width))
    call = functools.partial(
        attention, own=own, tenant=tenant, lengths=live_prefix_length, adapter_slot=tenant_adapter_slot,
        q=queries[0], grad=output_gradient[0], own_key=row_own_keys[0], own_value=row_own_values[0],
        adapters=query_up_adapters, mid_in=input_times_down[0],
    )
    dq, mid, up = call(first=0, pairs=pairs[0], earlier=())
    dq, terms = call(first=PART, pairs=pairs[1], earlier=(dq, mid, up, normed_layer_input[0]))
    terms = lax.all_to_all(terms, "bank", split_axis=0, concat_axis=0, tiled=True)
    sums = sum_terms(own, tenant, tenant_adapter_slot, terms)
    parts = [sums[0]] + [
        lax.ppermute(sums[k], "group", [(i, (i + k) % 4) for i in range(4)]) for k in range(1, 4)
    ]

    def total(columns):
        return sum(p[:, :, columns].astype(jnp.float32) for p in parts)

    return dq[None], total(slice(UP, UP + DOWN)), total(slice(0, UP))


def solution(mesh):
    rows = P(("group", "bank"), None, None)
    return jax.shard_map(
        body,
        mesh=mesh,
        in_specs=(rows,) * 6 + (P(None, ("group", "bank"), None),) * 2 + (P(),) * 5,
        out_specs=(rows, P("group", None, "bank"), P("group", None, "bank")),
        check_vma=False,
    )
```

```python
import functools
import math

import jax
import jax.numpy as jnp
from jax import lax
from jax.experimental import pallas as pl
from jax.experimental.pallas import tpu as pltpu
from jax.sharding import PartitionSpec as P

SEQ = 256
PREFIX = 2048
HEAD = 128
KV_HEADS = 4
GROUP = 8
RANK = 16
KEY_BLOCK = 256
BLOCKS = PREFIX // KEY_BLOCK
ALL_KEYS = PREFIX + SEQ
LEAST_LIVE = 512
SLOTS = 16
MASKED = -1e30
SCALE = HEAD**-0.5
SCALE2 = SCALE * math.log2(math.e)
ADAPTER_SCALE = 2.0
ROWS_AT_ONCE = 16
UP = 128
DOWN = 160
TERM = 384
BANKS = 32
PART = 2
PAIRS = GROUP // 2
WIDTH = PART * GROUP * HEAD


def lookup(table, position):
    matches = position[..., None] == jnp.arange(table.shape[0], dtype=jnp.int32)
    return jnp.sum(jnp.where(matches, table, 0), -1)


def dot(a, b, a_dim, b_dim):
    return lax.dot_general(
        a, b, (((a_dim,), (b_dim,)), ((), ())), preferred_element_type=jnp.float32
    )


def interleave(a, b):
    mixed, i, j = [], 0, 0
    while i < len(a) or j < len(b):
        if j == len(b) or (i < len(a) and i * len(b) <= j * len(a)):
            mixed.append(a[i])
            i += 1
        else:
            mixed.append(b[j])
            j += 1
    return mixed


def run(steps):
    for step in steps:
        step()


def attention_kernel(
    last,
    own, tenant, lengths, adapter_slot,
    q_ref, grad_ref, pairs_ref, own_key_ref, own_value_ref, adapter_ref, mid_in_ref,
    *refs,
):
    if last:
        _, mid_so_far, up_so_far, x_ref, dq_ref, term_ref, *scratch = refs
    else:
        dq_ref, mid_ref, up_ref, *scratch = refs
    scores0, scores1, probs0, probs1, grads0, grads1, bias, partial, down = scratch
    scores, probs, grads = (scores0, scores1), (probs0, probs1), (grads0, grads1)
    length = lengths[tenant[own[0]]]
    position = lax.broadcasted_iota(jnp.int32, bias.shape, 1)
    bias[...] = jnp.where(position < length, 0.0, MASKED)
    tiles = [(j, j + KEY_BLOCK) for j in range(0, ALL_KEYS, KEY_BLOCK)]

    def keys(p, a, b):
        h = p // PAIRS * HEAD
        return pairs_ref[a:b, h : h + HEAD] if a < PREFIX else own_key_ref[:, h : h + HEAD]

    def values(p, a, b):
        h = p // PAIRS * HEAD
        at = PART * HEAD + h
        return pairs_ref[a:b, at : at + HEAD] if a < PREFIX else own_value_ref[:, h : h + HEAD]

    def pair(ref, p):
        return jnp.concatenate(
            [ref[:, i * HEAD : (i + 1) * HEAD] for i in (2 * p, 2 * p + 1)], axis=0
        )

    def front(p, s):
        q, grad = pair(q_ref, p), pair(grad_ref, p)

        def score(a, b):
            scores[s][:, a:b] = dot(q, keys(p, a, b), 1, 1)

        def prob(a, b):
            probs[s][:, a:b] = dot(grad, values(p, a, b), 1, 1)

        return [functools.partial(f, a, b) for f in (score, prob) for a, b in tiles]

    def soft(s):
        def rows_at(r):
            rows = slice(r, r + ROWS_AT_ONCE)
            x = scores[s][rows, :]
            row = lax.broadcasted_iota(jnp.int32, (ROWS_AT_ONCE, SEQ), 0) + r % SEQ
            column = lax.broadcasted_iota(jnp.int32, (ROWS_AT_ONCE, SEQ), 1)
            x = jnp.concatenate(
                [
                    x[:, :LEAST_LIVE],
                    x[:, LEAST_LIVE:PREFIX] + bias[0:1, LEAST_LIVE:],
                    jnp.where(column <= row, x[:, PREFIX:], MASKED),
                ],
                axis=1,
            )
            top = jnp.max(x, axis=-1, keepdims=True)
            e = jnp.exp2(x * SCALE2 - top * SCALE2)
            inverse = 1.0 / jnp.sum(e, axis=-1, keepdims=True)
            prob_grad = probs[s][rows, :]
            delta = jnp.sum(e * prob_grad, axis=-1, keepdims=True) * inverse
            grads[s][rows, :] = ((e * inverse) * (prob_grad - delta)).astype(jnp.bfloat16)

        return [functools.partial(rows_at, r) for r in range(0, 2 * SEQ, ROWS_AT_ONCE)]

    def back(p, s):
        def part(i, a, b):
            x = dot(grads[s][:, a:b], keys(p, a, b), 1, 0)
            if i:
                x += partial[...]
            if b < ALL_KEYS:
                partial[...] = x
            else:
                store(p, x)

        return [functools.partial(part, i, a, b) for i, (a, b) in enumerate(tiles)]

    def store(p, x):
        x = (x * SCALE).astype(jnp.bfloat16)
        for k in range(2):
            dq_ref[:, (2 * p + k) * HEAD : (2 * p + k + 1) * HEAD] = x[k * SEQ : (k + 1) * SEQ]

    count = PART * PAIRS
    run(front(0, 0))
    for p in range(count):
        ahead = front(p + 1, (p + 1) % 2) if p + 1 < count else []
        behind = back(p - 1, (p - 1) % 2) if p else []
        run(interleave(behind + ahead, soft(p % 2)))
    end, s = count - 1, (count - 1) % 2
    x = dot(grads[s][:, :PREFIX], keys(end, 0, PREFIX), 1, 0)
    store(end, x + dot(grads[s][:, PREFIX:], keys(end, PREFIX, ALL_KEYS), 1, 0))

    dq = dq_ref[...]
    mid = dot(dq, adapter_ref[0], 1, 1)
    if last:
        mid += mid_so_far[...]
    up = (ADAPTER_SCALE * dot(mid_in_ref[...], dq, 0, 0)).astype(jnp.bfloat16)
    if last:
        down[...] = ADAPTER_SCALE * dot(mid.astype(jnp.bfloat16), x_ref[...], 0, 0)
    else:
        mid_ref[...] = mid
    for b in range(BANKS):
        i = b % (BANKS // 2)
        piece = up[:, i * UP : (i + 1) * UP]
        if last:
            term_ref[b, :, 0:UP] = up_so_far[i] if b == i else piece
            term_ref[b, :, UP : UP + DOWN] = down[:, b * DOWN : (b + 1) * DOWN].astype(jnp.bfloat16)
            term_ref[b, :, UP + DOWN :] = jnp.zeros((RANK, TERM - UP - DOWN), jnp.bfloat16)
        elif b == i:
            up_ref[i] = piece


def attention(first, own, tenant, lengths, adapter_slot, q, grad, pairs, own_key, own_value, adapters, mid_in, earlier):
    last = bool(earlier)

    def wide(shape):
        return pl.BlockSpec(shape, lambda g, *_: (0, first // PART))

    def whole(shape):
        return pl.BlockSpec(shape, lambda g, *_: (0,) * len(shape))

    def adapter_at(g, own, tenant, lengths, adapter_slot):
        return (adapter_slot[tenant[own[0]]], 0, first // PART)

    dq = jax.ShapeDtypeStruct(q.shape, jnp.bfloat16)
    if last:
        out_shape = (dq, jax.ShapeDtypeStruct((BANKS, RANK, TERM), jnp.bfloat16))
        out_specs = (wide((SEQ, WIDTH)), whole((BANKS, RANK, TERM)))
        more = [pl.BlockSpec(memory_space=pl.ANY)] + [whole(e.shape) for e in earlier[1:]]
    else:
        out_shape = (
            dq,
            jax.ShapeDtypeStruct((SEQ, RANK), jnp.float32),
            jax.ShapeDtypeStruct((BANKS // 2, RANK, UP), jnp.bfloat16),
        )
        out_specs = (
            wide((SEQ, WIDTH)),
            whole((SEQ, RANK)),
            whole((BANKS // 2, RANK, UP)),
        )
        more = []
    return pl.pallas_call(
        functools.partial(attention_kernel, last),
        out_shape=out_shape,
        grid_spec=pltpu.PrefetchScalarGridSpec(
            num_scalar_prefetch=4,
            grid=(1,),
            in_specs=[
                wide((SEQ, WIDTH)),
                wide((SEQ, WIDTH)),
                whole(pairs.shape),
                wide((SEQ, PART * HEAD)),
                wide((SEQ, PART * HEAD)),
                pl.BlockSpec((1, RANK, WIDTH), adapter_at),
                whole(mid_in.shape),
                *more,
            ],
            out_specs=out_specs,
            scratch_shapes=[
                *[pltpu.VMEM((2 * SEQ, ALL_KEYS), jnp.float32)] * 4,
                *[pltpu.VMEM((2 * SEQ, ALL_KEYS), jnp.bfloat16)] * 2,
                pltpu.VMEM((8, PREFIX), jnp.float32),
                pltpu.VMEM((2 * SEQ, HEAD), jnp.float32),
                pltpu.VMEM((RANK, BANKS * DOWN), jnp.float32),
            ],
        ),
        input_output_aliases={11: 0} if last else {},
        compiler_params=pltpu.CompilerParams(vmem_limit_bytes=56 << 20),
        cost_estimate=pl.CostEstimate(flops=15_000_000_000, bytes_accessed=8_000_000, transcendentals=10_000_000),
        name="attention_last" if last else "attention_first",
    )(own, tenant, lengths, adapter_slot, q, grad, pairs, own_key, own_value, adapters, mid_in, *earlier)


def sum_kernel(own, tenant, adapter_slot, terms_ref, a0_ref, a1_ref, a2_ref, a3_ref, total):
    total[...] = jnp.zeros_like(total)
    mine = own[0] // BANKS
    for i in range(BANKS):
        slot = adapter_slot[tenant[mine * BANKS + i]]
        total[slot] += terms_ref[i].astype(jnp.float32)
    for k, ref in enumerate((a0_ref, a1_ref, a2_ref, a3_ref)):
        start = lax.rem(mine + k, 4) * 4
        for i in range(4):
            ref[i] = total[start + i].astype(ref.dtype)


def sum_terms(own, tenant, adapter_slot, terms):
    shape = (4, RANK, TERM)
    return pl.pallas_call(
        sum_kernel,
        out_shape=[
            jax.ShapeDtypeStruct(shape, jnp.bfloat16 if k else jnp.float32) for k in range(4)
        ],
        grid_spec=pltpu.PrefetchScalarGridSpec(
            num_scalar_prefetch=3,
            grid=(1,),
            in_specs=[pl.BlockSpec(terms.shape, lambda i, *_: (0, 0, 0))],
            out_specs=[pl.BlockSpec(shape, lambda i, *_: (0, 0, 0))] * 4,
            scratch_shapes=[pltpu.VMEM((SLOTS, RANK, TERM), jnp.float32)],
        ),
        name="sum_terms",
    )(own, tenant, adapter_slot, terms)


def add_kernel(a0_ref, a1_ref, a2_ref, a3_ref, down_ref, up_ref):
    total = a0_ref[...]
    for ref in (a1_ref, a2_ref, a3_ref):
        total += ref[...].astype(jnp.float32)
    up_ref[...] = total[:, :, :UP]
    down_ref[...] = total[:, :, UP : UP + DOWN]


def add_groups(parts):
    shape = parts[0].shape[:2]
    return pl.pallas_call(
        add_kernel,
        out_shape=[jax.ShapeDtypeStruct((*shape, width), jnp.float32) for width in (DOWN, UP)],
        name="add_groups",
    )(*parts)


def body(
    normed_layer_input,
    input_times_down,
    queries,
    row_own_keys,
    row_own_values,
    output_gradient,
    prefix_key_bank,
    prefix_value_bank,
    live_prefix_length,
    tenant,
    tenant_bank_slot,
    tenant_adapter_slot,
    query_up_adapters,
):
    own = lax.axis_index(("group", "bank")).astype(jnp.int32)[None]
    bank_slot = lookup(tenant_bank_slot, tenant)
    width = PART * HEAD
    pairs = []
    for first in range(0, KV_HEADS, PART):
        columns = slice(first * HEAD, first * HEAD + width)
        share = jnp.concatenate([prefix_key_bank[:, :, columns], prefix_value_bank[:, :, columns]], -1)
        got = lax.all_to_all(share[bank_slot], ("group", "bank"), split_axis=0, concat_axis=0, tiled=True)
        pairs.append(got.reshape(PREFIX, 2 * width))
    call = functools.partial(
        attention, own=own, tenant=tenant, lengths=live_prefix_length, adapter_slot=tenant_adapter_slot,
        q=queries[0], grad=output_gradient[0], own_key=row_own_keys[0], own_value=row_own_values[0],
        adapters=query_up_adapters, mid_in=input_times_down[0],
    )
    dq, mid, up = call(first=0, pairs=pairs[0], earlier=())
    dq, terms = call(first=PART, pairs=pairs[1], earlier=(dq, mid, up, normed_layer_input[0]))
    terms = lax.all_to_all(terms, "bank", split_axis=0, concat_axis=0, tiled=True)
    sums = sum_terms(own, tenant, tenant_adapter_slot, terms)
    parts = [sums[0]] + [
        lax.ppermute(sums[k], "group", [(i, (i + k) % 4) for i in range(4)]) for k in range(1, 4)
    ]

    down_grad, up_grad = add_groups(parts)
    return dq[None], down_grad, up_grad


def solution(mesh):
    rows = P(("group", "bank"), None, None)
    return jax.shard_map(
        body,
        mesh=mesh,
        in_specs=(rows,) * 6 + (P(None, ("group", "bank"), None),) * 2 + (P(),) * 5,
        out_specs=(rows, P("group", None, "bank"), P("group", None, "bank")),
        check_vma=False,
    )
```

```python
import functools
import math

import jax
import jax.numpy as jnp
from jax import lax
from jax.experimental import pallas as pl
from jax.experimental.pallas import tpu as pltpu
from jax.sharding import PartitionSpec as P

SEQ = 256
PREFIX = 2048
HEAD = 128
KV_HEADS = 4
GROUP = 8
RANK = 16
KEY_BLOCK = 256
BLOCKS = PREFIX // KEY_BLOCK
ALL_KEYS = PREFIX + SEQ
LEAST_LIVE = 512
SLOTS = 16
MASKED = -1e30
SCALE = HEAD**-0.5
SCALE2 = SCALE * math.log2(math.e)
ADAPTER_SCALE = 2.0
ROWS_AT_ONCE = 16
UP = 128
DOWN = 160
TERM = 384
BANKS = 32
PART = 2


def lookup(table, position):
    matches = position[..., None] == jnp.arange(table.shape[0], dtype=jnp.int32)
    return jnp.sum(jnp.where(matches, table, 0), -1)


def dot(a, b, a_dim, b_dim):
    return lax.dot_general(
        a, b, (((a_dim,), (b_dim,)), ((), ())), preferred_element_type=jnp.float32
    )


def interleave(a, b):
    mixed, i, j = [], 0, 0
    while i < len(a) or j < len(b):
        if j == len(b) or (i < len(a) and i * len(b) <= j * len(a)):
            mixed.append(a[i])
            i += 1
        else:
            mixed.append(b[j])
            j += 1
    return mixed


def run(steps):
    for step in steps:
        step()


def attention_kernel(
    last,
    own, tenant, lengths, adapter_slot,
    q_ref, grad_ref, key_ref, value_ref, own_key_ref, own_value_ref, adapter_ref, mid_in_ref,
    *refs,
):
    if last:
        _, mid_so_far, up_so_far, x_ref, dq_ref, term_ref, *scratch = refs
    else:
        dq_ref, mid_ref, up_ref, *scratch = refs
    scores0, scores1, probs0, probs1, grads0, grads1, bias, partial, mid_sum, down = scratch
    g = pl.program_id(0)
    scores, probs, grads = (scores0, scores1), (probs0, probs1), (grads0, grads1)
    length = lengths[tenant[own[0]]]
    position = lax.broadcasted_iota(jnp.int32, bias.shape, 1)
    bias[...] = jnp.where(position < length, 0.0, MASKED)
    tiles = [(j, j + KEY_BLOCK) for j in range(0, ALL_KEYS, KEY_BLOCK)]

    def block(prefix_ref, own_ref, a, b):
        return prefix_ref[a:b, :] if a < PREFIX else own_ref[...]

    def pair(ref, p):
        return jnp.concatenate(
            [ref[:, i * HEAD : (i + 1) * HEAD] for i in (2 * p, 2 * p + 1)], axis=0
        )

    def front(p, s):
        q, grad = pair(q_ref, p), pair(grad_ref, p)

        def score(a, b):
            scores[s][:, a:b] = dot(q, block(key_ref, own_key_ref, a, b), 1, 1)

        def prob(a, b):
            probs[s][:, a:b] = dot(grad, block(value_ref, own_value_ref, a, b), 1, 1)

        return [functools.partial(f, a, b) for f in (score, prob) for a, b in tiles]

    def soft(s):
        def rows_at(r):
            rows = slice(r, r + ROWS_AT_ONCE)
            x = scores[s][rows, :]
            row = lax.broadcasted_iota(jnp.int32, (ROWS_AT_ONCE, SEQ), 0) + r % SEQ
            column = lax.broadcasted_iota(jnp.int32, (ROWS_AT_ONCE, SEQ), 1)
            x = jnp.concatenate(
                [
                    x[:, :LEAST_LIVE],
                    x[:, LEAST_LIVE:PREFIX] + bias[0:1, LEAST_LIVE:],
                    jnp.where(column <= row, x[:, PREFIX:], MASKED),
                ],
                axis=1,
            )
            top = jnp.max(x, axis=-1, keepdims=True)
            e = jnp.exp2(x * SCALE2 - top * SCALE2)
            inverse = 1.0 / jnp.sum(e, axis=-1, keepdims=True)
            prob_grad = probs[s][rows, :]
            delta = jnp.sum(e * prob_grad, axis=-1, keepdims=True) * inverse
            grads[s][rows, :] = ((e * inverse) * (prob_grad - delta)).astype(jnp.bfloat16)

        return [functools.partial(rows_at, r) for r in range(0, 2 * SEQ, ROWS_AT_ONCE)]

    def back(p, s):
        def part(i, a, b):
            x = dot(grads[s][:, a:b], block(key_ref, own_key_ref, a, b), 1, 0)
            if i:
                x += partial[...]
            if b < ALL_KEYS:
                partial[...] = x
            else:
                x = (x * SCALE).astype(jnp.bfloat16)
                for k in range(2):
                    dq_ref[:, (2 * p + k) * HEAD : (2 * p + k + 1) * HEAD] = x[k * SEQ : (k + 1) * SEQ]

        return [functools.partial(part, i, a, b) for i, (a, b) in enumerate(tiles)]

    run(front(0, 0))
    run(interleave(front(1, 1), soft(0)))
    run(interleave(back(0, 0) + front(2, 0), soft(1)))
    run(interleave(back(1, 1) + front(3, 1), soft(0)))
    run(interleave(back(2, 0), soft(1)))
    x = dot(grads1[:, :PREFIX], key_ref[...], 1, 0) + dot(grads1[:, PREFIX:], own_key_ref[...], 1, 0)
    x = (x * SCALE).astype(jnp.bfloat16)
    for k in range(2):
        dq_ref[:, (6 + k) * HEAD : (7 + k) * HEAD] = x[k * SEQ : (k + 1) * SEQ]

    @pl.when(g == 0)
    def _():
        mid_sum[...] = mid_so_far[...] if last else jnp.zeros_like(mid_sum)

    dq = dq_ref[...]
    mid_sum[...] += dot(dq, adapter_ref[0], 1, 1)
    up = (ADAPTER_SCALE * dot(mid_in_ref[...], dq, 0, 0)).astype(jnp.bfloat16)
    for i in range(GROUP):
        piece = up[:, i * UP : (i + 1) * UP]
        if last:
            term_ref[BANKS // 2 + g * GROUP + i, :, 0:UP] = piece
        else:
            up_ref[i] = piece

    @pl.when(g == PART - 1)
    def _():
        if last:
            mid = mid_sum[...].astype(jnp.bfloat16)
            down[...] = ADAPTER_SCALE * dot(mid, x_ref[...], 0, 0)
            for b in range(BANKS):
                if b < BANKS // 2:
                    term_ref[b, :, 0:UP] = up_so_far[b]
                term_ref[b, :, UP : UP + DOWN] = down[:, b * DOWN : (b + 1) * DOWN].astype(jnp.bfloat16)
                term_ref[b, :, UP + DOWN :] = jnp.zeros((RANK, TERM - UP - DOWN), jnp.bfloat16)
        else:
            mid_ref[...] = mid_sum[...]


def attention(first, own, tenant, lengths, adapter_slot, q, grad, pairs, own_key, own_value, adapters, mid_in, earlier):
    last = bool(earlier)

    def wide(shape):
        return pl.BlockSpec(shape, lambda g, *_: (0, first + g))

    def whole(shape):
        return pl.BlockSpec(shape, lambda g, *_: (0,) * len(shape))

    def adapter_at(g, own, tenant, lengths, adapter_slot):
        return (adapter_slot[tenant[own[0]]], 0, first + g)

    dq = jax.ShapeDtypeStruct(q.shape, jnp.bfloat16)
    if last:
        out_shape = (dq, jax.ShapeDtypeStruct((BANKS, RANK, TERM), jnp.bfloat16))
        out_specs = (wide((SEQ, GROUP * HEAD)), whole((BANKS, RANK, TERM)))
        more = [pl.BlockSpec(memory_space=pl.ANY)] + [whole(e.shape) for e in earlier[1:]]
    else:
        out_shape = (
            dq,
            jax.ShapeDtypeStruct((SEQ, RANK), jnp.float32),
            jax.ShapeDtypeStruct((BANKS // 2, RANK, UP), jnp.bfloat16),
        )
        out_specs = (
            wide((SEQ, GROUP * HEAD)),
            whole((SEQ, RANK)),
            pl.BlockSpec((GROUP, RANK, UP), lambda g, *_: (g, 0, 0)),
        )
        more = []
    return pl.pallas_call(
        functools.partial(attention_kernel, last),
        out_shape=out_shape,
        grid_spec=pltpu.PrefetchScalarGridSpec(
            num_scalar_prefetch=4,
            grid=(PART,),
            in_specs=[
                wide((SEQ, GROUP * HEAD)),
                wide((SEQ, GROUP * HEAD)),
                pl.BlockSpec((PREFIX, HEAD), lambda g, *_: (0, g)),
                pl.BlockSpec((PREFIX, HEAD), lambda g, *_: (0, PART + g)),
                wide((SEQ, HEAD)),
                wide((SEQ, HEAD)),
                pl.BlockSpec((1, RANK, GROUP * HEAD), adapter_at),
                whole(mid_in.shape),
                *more,
            ],
            out_specs=out_specs,
            scratch_shapes=[
                *[pltpu.VMEM((2 * SEQ, ALL_KEYS), jnp.float32)] * 4,
                *[pltpu.VMEM((2 * SEQ, ALL_KEYS), jnp.bfloat16)] * 2,
                pltpu.VMEM((8, PREFIX), jnp.float32),
                pltpu.VMEM((2 * SEQ, HEAD), jnp.float32),
                pltpu.VMEM((SEQ, RANK), jnp.float32),
                pltpu.VMEM((RANK, BANKS * DOWN), jnp.float32),
            ],
        ),
        input_output_aliases={12: 0} if last else {},
        compiler_params=pltpu.CompilerParams(vmem_limit_bytes=56 << 20),
        cost_estimate=pl.CostEstimate(flops=15_000_000_000, bytes_accessed=8_000_000, transcendentals=10_000_000),
        name="attention_last" if last else "attention_first",
    )(own, tenant, lengths, adapter_slot, q, grad, pairs, pairs, own_key, own_value, adapters, mid_in, *earlier)


def sum_kernel(own, tenant, adapter_slot, terms_ref, a0_ref, a1_ref, a2_ref, a3_ref, total):
    total[...] = jnp.zeros_like(total)
    mine = own[0] // BANKS
    for i in range(BANKS):
        slot = adapter_slot[tenant[mine * BANKS + i]]
        total[slot] += terms_ref[i].astype(jnp.float32)
    for k, ref in enumerate((a0_ref, a1_ref, a2_ref, a3_ref)):
        start = lax.rem(mine + k, 4) * 4
        for i in range(4):
            ref[i] = total[start + i].astype(ref.dtype)


def sum_terms(own, tenant, adapter_slot, terms):
    shape = (4, RANK, TERM)
    return pl.pallas_call(
        sum_kernel,
        out_shape=[
            jax.ShapeDtypeStruct(shape, jnp.bfloat16 if k else jnp.float32) for k in range(4)
        ],
        grid_spec=pltpu.PrefetchScalarGridSpec(
            num_scalar_prefetch=3,
            grid=(1,),
            in_specs=[pl.BlockSpec(terms.shape, lambda i, *_: (0, 0, 0))],
            out_specs=[pl.BlockSpec(shape, lambda i, *_: (0, 0, 0))] * 4,
            scratch_shapes=[pltpu.VMEM((SLOTS, RANK, TERM), jnp.float32)],
        ),
        name="sum_terms",
    )(own, tenant, adapter_slot, terms)


def add_kernel(a0_ref, a1_ref, a2_ref, a3_ref, down_ref, up_ref):
    total = a0_ref[...]
    for ref in (a1_ref, a2_ref, a3_ref):
        total += ref[...].astype(jnp.float32)
    up_ref[...] = total[:, :, :UP]
    down_ref[...] = total[:, :, UP : UP + DOWN]


def add_groups(parts):
    shape = parts[0].shape[:2]
    return pl.pallas_call(
        add_kernel,
        out_shape=[jax.ShapeDtypeStruct((*shape, width), jnp.float32) for width in (DOWN, UP)],
        name="add_groups",
    )(*parts)


def body(
    normed_layer_input,
    input_times_down,
    queries,
    row_own_keys,
    row_own_values,
    output_gradient,
    prefix_key_bank,
    prefix_value_bank,
    live_prefix_length,
    tenant,
    tenant_bank_slot,
    tenant_adapter_slot,
    query_up_adapters,
):
    own = lax.axis_index(("group", "bank")).astype(jnp.int32)[None]
    bank_slot = lookup(tenant_bank_slot, tenant)
    width = PART * HEAD
    pairs = []
    for first in range(0, KV_HEADS, PART):
        columns = slice(first * HEAD, first * HEAD + width)
        share = jnp.concatenate([prefix_key_bank[:, :, columns], prefix_value_bank[:, :, columns]], -1)
        got = lax.all_to_all(share[bank_slot], ("group", "bank"), split_axis=0, concat_axis=0, tiled=True)
        pairs.append(got.reshape(PREFIX, 2 * width))
    call = functools.partial(
        attention, own=own, tenant=tenant, lengths=live_prefix_length, adapter_slot=tenant_adapter_slot,
        q=queries[0], grad=output_gradient[0], own_key=row_own_keys[0], own_value=row_own_values[0],
        adapters=query_up_adapters, mid_in=input_times_down[0],
    )
    dq, mid, up = call(first=0, pairs=pairs[0], earlier=())
    dq, terms = call(first=PART, pairs=pairs[1], earlier=(dq, mid, up, normed_layer_input[0]))
    terms = lax.all_to_all(terms, "bank", split_axis=0, concat_axis=0, tiled=True)
    sums = sum_terms(own, tenant, tenant_adapter_slot, terms)
    parts = [sums[0]] + [
        lax.ppermute(sums[k], "group", [(i, (i + k) % 4) for i in range(4)]) for k in range(1, 4)
    ]

    down_grad, up_grad = add_groups(parts)
    return dq[None], down_grad, up_grad


def solution(mesh):
    rows = P(("group", "bank"), None, None)
    return jax.shard_map(
        body,
        mesh=mesh,
        in_specs=(rows,) * 6 + (P(None, ("group", "bank"), None),) * 2 + (P(),) * 5,
        out_specs=(rows, P("group", None, "bank"), P("group", None, "bank")),
        check_vma=False,
    )
```
